256 devices in a mesh: layer: 32 (over z, y_lo, core), rep: 8 (over y_hi, x).
Axes of the slice: x: 4, y: 4 (y_hi: 2, y_lo: 2; y = y_hi * 2 + y_lo), z: 8, core: 2. Of those that a mesh axis runs over, the one named last changes fastest.
Arguments:
- features: bfloat16 [32768, 512], P(('layer', 'rep')), may hold values from -6 to 6
- block_columns: int32 [256, 128], P('layer', 'rep'), may hold values from -1 to 255, as said below
- block_values: int32 [256, 128, 128, 128], P('layer', 'rep'), may hold values from 0 to 3, as said below
- weight: bfloat16 [512, 512], replicated, may hold values from -1.5 to 1.5
- bias_row: float32 [512], replicated, may hold values from -3 to 3
- cotangent: bfloat16 [32768, 512], P(('layer', 'rep')), may hold values from -6 to 6
Outputs:
- activations: bfloat16 [32768, 512], P(('layer', 'rep'))
- weight_grad: float32 [512, 512], replicated
- bias_grad: float32 [512], replicated
- feature_grad: bfloat16 [32768, 512], P(('layer', 'rep'))
The draws below stay inside these ranges and needn't reach their ends.
Inputs may be any that keep to these rules, and one draw needn't show every extreme that they name: `block_columns`: in row panel p, slots r*16 to (r+1)*16 - 1 name distinct column blocks in rising order, each inside a span of 128 nodes whose span index is r modulo 8; the used slots come first, at least one in each such group, and the others hold -1. Some group of some row panel uses all 16 slots in every draw. `block_values`: zero in every slot whose column is -1.
All inputs are finite; a program needn't handle non-finite values.
Results may differ from the reference program's by a relative error of at most 0.007.
Values may be sent and summed in bfloat16 or wider, within the bound.
No kernel may reach another device: no remote copies, remote signals or barrier semaphores. Data moves between devices by JAX's collectives and lax.ppermute only.
A program may use at most 128 MiB of HBM per device.

```python
import jax
import jax.numpy as jnp
from jax import lax

F = 512
BLK = 128
MAXB = 16
RD = 128
NODES = 32768
PANELS = 256
N_LAYER = 32
N_REP = 8


def slot_layout(key):
    span_blocks = RD // BLK
    section_count = N_LAYER * span_blocks
    panels_layer = PANELS // N_LAYER
    key_level, key_drop, key_score, key_force = jax.random.split(key, 4)
    level_index = jax.random.randint(key_level, (N_LAYER, 1, 1), 0, 3)
    base_count = MAXB - level_index * (MAXB // 4)
    base_count = jnp.broadcast_to(base_count, (N_LAYER, panels_layer, N_REP)).reshape(PANELS, N_REP)
    dropped = jax.random.randint(key_drop, (PANELS, N_REP), 0, 1 << 20) % (base_count // 4 + 1)
    counts = base_count - dropped
    forced = jax.random.randint(key_force, (), 0, PANELS)
    panel_ids = jnp.arange(PANELS, dtype=jnp.int32)[:, None]
    rep_ids = jnp.arange(N_REP, dtype=jnp.int32)[None, :]
    is_forced = (panel_ids == forced) & (rep_ids == N_REP - 1)
    counts = jnp.where(is_forced, MAXB, counts)
    block_ids = jnp.arange(section_count, dtype=jnp.int32)
    scores = jax.random.randint(key_score, (PANELS, N_REP, section_count), 0, 1 << 20)
    scores = scores * section_count + block_ids
    scores = jnp.where(is_forced[:, :, None] & (block_ids == section_count - 1), (1 << 20) * section_count, scores)
    ordering = jnp.argsort(-scores, axis=-1)
    ranking = jnp.argsort(ordering, axis=-1)
    chosen = ranking < counts[:, :, None]
    position = jnp.cumsum(chosen.astype(jnp.int32), axis=-1) - 1
    target = jnp.where(chosen, position, MAXB)
    layer_index = block_ids // span_blocks
    within = block_ids % span_blocks
    global_ids = ((layer_index * N_REP)[None, None, :] + rep_ids[:, :, None]) * span_blocks + within[None, None, :]
    global_ids = jnp.broadcast_to(global_ids, target.shape)
    panel_axis = jnp.arange(PANELS, dtype=jnp.int32)[:, None, None]
    rep_axis = jnp.arange(N_REP, dtype=jnp.int32)[None, :, None]
    columns = jnp.full((PANELS, N_REP, MAXB + 1), -1, jnp.int32)
    columns = columns.at[panel_axis, rep_axis, target].set(global_ids)
    return columns[:, :, :MAXB].reshape(PANELS, N_REP * MAXB)


def draw_block_columns(key, part):
    columns = slot_layout(key)
    return columns


def draw_block_values(key, part):
    columns = slot_layout(key)
    key = jax.random.fold_in(key, 12)
    raw_draw = jax.random.randint(key, (PANELS, N_REP * MAXB, BLK, BLK), 0, 6 * BLK)
    values = jnp.where(raw_draw < 3, raw_draw + 1, 0)
    used_slot = (columns >= 0)[:, :, None, None]
    return jnp.where(used_slot, values, 0).astype(jnp.int32)


def block_levels(own_key, extent, cuts, low, largest):
    level = 1.0
    for dim, blocks in cuts:
        steps = jax.random.uniform(jax.random.fold_in(jax.random.fold_in(own_key, 6), dim), (blocks,), jnp.float32, low / len(cuts), largest / len(cuts))
        level = level * jnp.repeat(jnp.exp(steps), extent[dim] // blocks).reshape((-1,) + (1,) * (len(extent) - 1 - dim))
    return level


def normal_values(own_key, extent, width, reach, cuts=(), kind=jnp.bfloat16):
    array = width * jax.random.normal(own_key, extent, jnp.float32)
    if cuts:
        array = array * block_levels(own_key, extent, cuts, -0.22, 0.18)
    return jnp.clip(array, -reach, reach).astype(kind)


def setup_inputs(seed: int = 0) -> dict:
    splits = jax.random.split(jax.random.key(seed), 7)
    return {
        "features": normal_values(splits[0], (NODES, F), 1.0, 6.0, ((0, 256),)),
        "block_columns": draw_block_columns(jax.random.fold_in(splits[6], 71), 0),
        "block_values": draw_block_values(jax.random.fold_in(splits[6], 71), 0),
        "weight": normal_values(splits[3], (F, F), (F // 32) ** -0.5, 1.5),
        "bias_row": normal_values(splits[4], (F,), 0.5, 3.0, (), jnp.float32),
        "cotangent": normal_values(splits[5], (NODES, F), 1.0, 6.0, ((0, 256),)),
    }


def reference(features, block_columns, block_values, weight, bias_row, cotangent):
    panel_count, slot_count = block_columns.shape
    block_edge = block_values.shape[2]
    node_count, feature_width = features.shape
    used_slot = block_columns >= 0
    safe_columns = jnp.where(used_slot, block_columns, 0).astype(jnp.int32)
    degree = 1.0 + jnp.sum(block_values, axis=(1, 3)).reshape(node_count).astype(jnp.float32)
    feature_blocks = features.reshape(panel_count, block_edge, feature_width)

    def panel_forward(inputs):
        columns, values = inputs
        gathered = feature_blocks[columns].astype(jnp.float32)
        return jnp.einsum("sij,sjf->if", values.astype(jnp.float32), gathered)

    neighbours = lax.map(panel_forward, (safe_columns, block_values))
    aggregate = neighbours.reshape(node_count, feature_width) + features.astype(jnp.float32)
    hidden = (aggregate / degree[:, None]).astype(jnp.bfloat16)
    preact = jnp.dot(hidden, weight, preferred_element_type=jnp.float32) + bias_row
    gate_value = jax.nn.sigmoid(preact)
    activations = (preact * gate_value).astype(jnp.bfloat16)
    slope = (cotangent.astype(jnp.float32) * gate_value * (1.0 + preact * (1.0 - gate_value))).astype(jnp.bfloat16)
    weight_grad = jnp.dot(hidden.T, slope, preferred_element_type=jnp.float32)
    bias_grad = jnp.sum(slope.astype(jnp.float32), axis=0)
    backward_rows = jnp.dot(slope, weight.T, preferred_element_type=jnp.float32)
    scaled = (backward_rows / degree[:, None]).astype(jnp.bfloat16)
    scaled_blocks = scaled.reshape(panel_count, block_edge, feature_width).astype(jnp.float32)

    def panel_backward(totals, inputs):
        columns, values, tile_rows = inputs
        contrib = jnp.einsum("sij,if->sjf", values.astype(jnp.float32), tile_rows)
        return totals.at[columns].add(contrib), None

    start_totals = jnp.zeros((panel_count, block_edge, feature_width), jnp.float32)
    spread, _ = lax.scan(panel_backward, start_totals, (safe_columns, block_values, scaled_blocks))
    feature_grad = (spread.reshape(node_count, feature_width) + scaled.astype(jnp.float32)).astype(jnp.bfloat16)
    return (activations, weight_grad, bias_grad, feature_grad)
```

```python
import functools

import jax
import jax.numpy as jnp
from jax import lax
from jax.experimental import pallas as pl
from jax.experimental.pallas import tpu as pltpu
from jax.sharding import PartitionSpec as P

BF = jnp.bfloat16
F32 = jnp.float32
Z, Y, C = 8, 2, 2
REPS = 8
BLK = 128
SLOTS = 16
F = 512
GROUPS = 8
DEG = 16


def layer_perm(dz, dy, dc):
    pairs = []
    for z in range(Z):
        for y in range(Y):
            for c in range(C):
                to = (((z + dz) % Z) * Y + (y + dy) % Y) * C + (c + dc) % C
                pairs.append(((z * Y + y) * C + c, to))
    return pairs


UP = layer_perm(1, 0, 0)
DOWN = layer_perm(-1, 0, 0)
SIDE = layer_perm(0, 1, 0)
CORE = layer_perm(0, 0, 1)


def send(value, perm):
    return lax.ppermute(value, "layer", perm)


def spread_kernel(place_ref, values_ref, dense_ref, degree_ref):
    panel = pl.program_id(0)
    dense_ref[...] = jnp.zeros_like(dense_ref)
    total = jnp.zeros((BLK, BLK), jnp.int32)
    for slot in range(SLOTS):
        tile = values_ref[0, slot]
        total = total + tile
        place = place_ref[panel * SLOTS + slot]

        @pl.when(place >= 0)
        def _():
            lane = pl.multiple_of((place % 4) * BLK, BLK)
            dense_ref[place // 4, :, pl.ds(lane, BLK)] = tile.astype(F32).astype(BF)

    row = lax.dot_general(
        jnp.ones((DEG, BLK), BF),
        total.astype(F32).astype(BF),
        (((1,), (1,)), ((), ())),
        preferred_element_type=F32,
    )
    high = jnp.floor(row * (1.0 / 128.0)) * 128.0
    degree_ref[...] = jnp.zeros_like(degree_ref)
    degree_ref[0, :, 0:BLK] = high.astype(BF)
    degree_ref[0, :, BLK : 2 * BLK] = (row - high).astype(BF)


def spread_blocks(place, values):
    panels = values.shape[0]
    return pl.pallas_call(
        spread_kernel,
        grid_spec=pltpu.PrefetchScalarGridSpec(
            num_scalar_prefetch=1,
            grid=(panels,),
            in_specs=[pl.BlockSpec((1, SLOTS, BLK, BLK), lambda p, place: (p, 0, 0, 0))],
            out_specs=[
                pl.BlockSpec((GROUPS, BLK, 4 * BLK), lambda p, place: (0, p, 0)),
                pl.BlockSpec((1, DEG, F), lambda p, place: (p, 0, 0)),
            ],
        ),
        out_shape=[
            jax.ShapeDtypeStruct((GROUPS, panels * BLK, 4 * BLK), BF),
            jax.ShapeDtypeStruct((panels, DEG, F), BF),
        ],
        compiler_params=pltpu.CompilerParams(vmem_limit_bytes=24 << 20),
        cost_estimate=pl.CostEstimate(flops=1 << 22, bytes_accessed=16 << 20, transcendentals=0),
    )(place.reshape(-1), values)


def node_kernel(
    got_ref, features_ref, weight_ref, bias_ref, cotangent_ref, act_ref, out_ref, scaled_ref
):
    got = got_ref[...].astype(F32)
    summed = jnp.sum(got, axis=0)
    parts = summed[BLK : BLK + 1, :]
    degree_row = 1.0 + parts[:, 0:BLK] + parts[:, BLK : 2 * BLK]
    degree = jnp.transpose(jnp.broadcast_to(degree_row, (BLK, BLK)))
    degree = jnp.concatenate([degree] * 4, axis=1)
    aggregate = summed[0:BLK] + features_ref[...].astype(F32)
    hidden_wide = (aggregate / degree).astype(BF)
    weight = weight_ref[...]
    preact = jnp.dot(hidden_wide, weight, preferred_element_type=F32) + bias_ref[...]
    gate = jax.nn.sigmoid(preact)
    act_ref[...] = (preact * gate).astype(BF)
    slope = (cotangent_ref[...].astype(F32) * gate * (1.0 + preact * (1.0 - gate))).astype(BF)
    rows = lax.dot_general(slope, weight, (((1,), (1,)), ((), ())), preferred_element_type=F32)
    scaled = (rows / degree).astype(BF)
    scaled_t = jnp.transpose(scaled.astype(F32)).astype(BF)
    scaled_ref[...] = scaled_t
    hidden_t = jnp.transpose(hidden_wide.astype(F32)).astype(BF)
    grad = jnp.dot(hidden_t, slope, preferred_element_type=F32).astype(BF)
    bias = jnp.sum(slope.astype(F32), axis=0, keepdims=True).astype(BF)
    out_ref[:, 768:784, :] = jnp.zeros((REPS, 16, BLK), BF)
    for peer in range(REPS):
        out_ref[peer, 0:512, :] = scaled_t
        for b in range(4):
            out_ref[peer, 512 + 64 * b : 576 + 64 * b, :] = grad[
                64 * peer : 64 * peer + 64, BLK * b : BLK * (b + 1)
            ]
            out_ref[peer, 768 + b : 769 + b, :] = bias[:, BLK * b : BLK * (b + 1)]


def node_step(got, features, weight, bias_row, cotangent):
    return pl.pallas_call(
        node_kernel,
        out_shape=[
            jax.ShapeDtypeStruct((BLK, F), BF),
            jax.ShapeDtypeStruct((REPS, 784, BLK), BF),
            jax.ShapeDtypeStruct((F, BLK), BF),
        ],
        compiler_params=pltpu.CompilerParams(vmem_limit_bytes=24 << 20),
        cost_estimate=pl.CostEstimate(
            flops=6 * BLK * F * F, bytes_accessed=4 << 20, transcendentals=BLK * F
        ),
    )(got, features, weight, bias_row.reshape(1, F), cotangent)


def per_device(features, block_columns, block_values, weight, bias_row, cotangent):
    layer = lax.axis_index("layer")
    z, y, c = layer // 4, (layer // 2) % 2, layer % 2
    owner = jnp.where(block_columns >= 0, block_columns, 0) // REPS
    dz = (owner // 4 - z + Z) % Z
    dy = ((owner // 2) % 2 - y) % 2
    dc = (owner % 2 - c) % 2
    near = jnp.where(dz <= 4, dz, Z - dz)
    is_up = (dz > 4).astype(jnp.int32)
    ends = (near == 0) | (near == 4)
    group = jnp.where(near == 0, 0, jnp.where(near == 4, 7, 2 * near - 1 + dc))
    column = jnp.where(ends, 2 * dc + dy, 2 * dy + 1 - is_up)
    place = jnp.where(block_columns >= 0, 4 * group + column, -1).astype(jnp.int32)
    dense, degree_rows = spread_blocks(place, block_values)

    arrived = []

    def finish(piece):
        both = jnp.concatenate([piece, send(piece, SIDE)], axis=0)
        return both, send(both, CORE)

    arrived.append(jnp.concatenate(finish(features), axis=0))
    up = down = features
    for _ in range(3):
        up, down = send(up, UP), send(down, DOWN)
        arrived.extend(finish(jnp.concatenate([up, down], axis=0)))
    half = BLK // 2
    last = jnp.concatenate([send(up[:half], UP), send(down[half:], DOWN)], axis=0)
    arrived.append(jnp.concatenate(finish(last), axis=0))
    partial = sum(
        jnp.dot(dense[g], arrived[g], preferred_element_type=F32) for g in range(GROUPS)
    )
    payload = jnp.concatenate([partial.reshape(REPS, BLK, F).astype(BF), degree_rows], axis=1)
    got = lax.all_to_all(payload, "rep", 0, 0, tiled=True)

    activations, outgoing, scaled_t = node_step(got, features, weight, bias_row, cotangent)
    everyone = lax.all_to_all(outgoing, "rep", 0, 0, tiled=True)
    wide = jnp.transpose(everyone[:, 0:F, :], (1, 0, 2)).reshape(F, REPS * BLK)
    grads = jnp.sum(everyone[:, F:, :].astype(F32), axis=0)

    def product(g):
        return jnp.dot(wide, dense[g], preferred_element_type=F32)

    def over_quad(mine, other):
        line = mine + send(other.astype(BF), CORE).astype(F32)
        width = line.shape[1] // 2
        return line[:, :width] + send(line[:, width:].astype(BF), SIDE).astype(F32)

    grads = grads + send(grads.astype(BF), CORE).astype(F32)
    grads = grads + send(grads.astype(BF), SIDE).astype(F32)
    grads_up = grads_down = grads.astype(BF)
    grad_total = grads

    def ends_quad(g):
        whole = product(g)
        return over_quad(whole[:, : 2 * BLK], whole[:, 2 * BLK :])

    far = ends_quad(7)
    top = F // 2
    from_up = send(far[:top].astype(BF), DOWN).astype(F32)
    from_down = send(far[top:].astype(BF), UP).astype(F32)
    pad = jnp.zeros((top, BLK), F32)
    from_up = jnp.concatenate([from_up, pad], axis=0)
    from_down = jnp.concatenate([pad, from_down], axis=0)
    for step in (3, 2, 1):
        quad = over_quad(product(2 * step - 1), product(2 * step))
        go_down = (quad[:, :BLK] + from_up).astype(BF)
        go_up = (quad[:, BLK:] + from_down).astype(BF)
        came_up = send(jnp.concatenate([go_down, grads_down], axis=0), DOWN)
        came_down = send(jnp.concatenate([go_up, grads_up], axis=0), UP)
        from_up, from_down = came_up[:F].astype(F32), came_down[:F].astype(F32)
        grads_down, grads_up = came_up[F:], came_down[F:]
        grad_total = grad_total + grads_down.astype(F32) + grads_up.astype(F32)
    last_up = send(grads_up[:BLK], UP)
    last_down = send(grads_down[BLK:], DOWN)
    grad_total = grad_total + jnp.concatenate([last_up, last_down], axis=0).astype(F32)
    spread = ends_quad(0) + from_up + from_down + scaled_t.astype(F32)
    feature_grad = jnp.transpose(spread).astype(BF)

    bias_grad = grad_total[256:260].reshape(F)
    mine = jnp.broadcast_to(grad_total[:256].astype(BF)[None], (REPS, 256, BLK))
    pieces = lax.all_to_all(mine, "rep", 0, 0, tiled=True)
    weight_grad = (
        pieces.reshape(REPS, 4, 64, BLK).transpose(0, 2, 1, 3).reshape(F, F).astype(F32)
    )
    return (activations, weight_grad, bias_grad, feature_grad)


def solution(mesh):
    in_specs = (
        P(("layer", "rep"), None),
        P("layer", "rep"),
        P("layer", "rep", None, None),
        P(),
        P(),
        P(("layer", "rep"), None),
    )
    out_specs = (P(("layer", "rep"), None), P(), P(), P(("layer", "rep"), None))
    return jax.shard_map(
        per_device, mesh=mesh, in_specs=in_specs, out_specs=out_specs, check_vma=False
    )
```

```python
import functools

import jax
import jax.numpy as jnp
from jax import lax
from jax.experimental import pallas as pl
from jax.experimental.pallas import tpu as pltpu
from jax.sharding import PartitionSpec as P

BF = jnp.bfloat16
F32 = jnp.float32
Z, Y, C = 8, 2, 2
REPS = 8
BLK = 128
SLOTS = 16
F = 512
GROUPS = 8
DEG = 16
ROWS = 800
HALF = 144


def layer_perm(dz, dy, dc):
    pairs = []
    for z in range(Z):
        for y in range(Y):
            for c in range(C):
                to = (((z + dz) % Z) * Y + (y + dy) % Y) * C + (c + dc) % C
                pairs.append(((z * Y + y) * C + c, to))
    return pairs


def core_perm(hops):
    pairs = []
    for z in range(Z):
        for y in range(Y):
            for c in range(C):
                step = hops if c == 0 else -hops
                pairs.append(((z * Y + y) * C + c, (((z + step) % Z) * Y + y) * C + c))
    return pairs


OUT1, OUT2 = core_perm(1), core_perm(2)
BACK1, BACK2 = core_perm(-1), core_perm(-2)
SIDE = layer_perm(0, 1, 0)
CORE = layer_perm(0, 0, 1)

def send(value, perm):
    return lax.ppermute(value, "layer", perm)


def after(value, *earlier):
    return lax.optimization_barrier((value,) + earlier)[0]


def spread_kernel(place_ref, values_ref, dense_ref, degree_ref, tiles, sems):
    panel = pl.program_id(0)

    def fetch(p):
        return pltpu.make_async_copy(values_ref.at[p], tiles.at[p], sems.at[p])

    @pl.when(panel == 0)
    def _():
        for p in range(REPS):
            fetch(p).start()

    dense_ref[...] = jnp.zeros_like(dense_ref)
    fetch(panel).wait()
    total = jnp.zeros((BLK, BLK), jnp.int32)
    for slot in range(SLOTS):
        tile = tiles[panel, slot]
        total = total + tile
        place = place_ref[panel * SLOTS + slot]

        @pl.when(place >= 0)
        def _():
            lane = pl.multiple_of((place % 4) * BLK, BLK)
            dense_ref[place // 4, :, pl.ds(lane, BLK)] = tile.astype(F32).astype(BF)

    row = lax.dot_general(
        jnp.ones((DEG, BLK), BF),
        total.astype(F32).astype(BF),
        (((1,), (1,)), ((), ())),
        preferred_element_type=F32,
    )
    high = jnp.floor(row * (1.0 / 128.0)) * 128.0
    degree_ref[...] = jnp.zeros_like(degree_ref)
    degree_ref[0, :, 0:BLK] = high.astype(BF)
    degree_ref[0, :, BLK : 2 * BLK] = (row - high).astype(BF)


def spread_blocks(place, values):
    panels = values.shape[0]
    return pl.pallas_call(
        spread_kernel,
        grid_spec=pltpu.PrefetchScalarGridSpec(
            num_scalar_prefetch=1,
            grid=(panels,),
            in_specs=[pl.BlockSpec(memory_space=pltpu.HBM)],
            out_specs=[
                pl.BlockSpec((GROUPS, BLK, 4 * BLK), lambda p, place: (0, p, 0)),
                pl.BlockSpec((1, DEG, F), lambda p, place: (p, 0, 0)),
            ],
            scratch_shapes=[
                pltpu.VMEM((panels, SLOTS, BLK, BLK), jnp.int32),
                pltpu.SemaphoreType.DMA((panels,)),
            ],
        ),
        out_shape=[
            jax.ShapeDtypeStruct((GROUPS, panels * BLK, 4 * BLK), BF),
            jax.ShapeDtypeStruct((panels, DEG, F), BF),
        ],
        compiler_params=pltpu.CompilerParams(vmem_limit_bytes=16 << 20),
        cost_estimate=pl.CostEstimate(flops=1 << 22, bytes_accessed=16 << 20, transcendentals=0),
    )(place.reshape(-1), pltpu.with_memory_space_constraint(values, pltpu.HBM))


def payload_kernel(total_ref, dense_ref, last_ref, degree_ref, out_ref):
    product = jnp.dot(dense_ref[0], last_ref[...], preferred_element_type=F32)
    out_ref[0, 0:BLK, :] = (total_ref[...] + product).astype(BF)
    out_ref[0, BLK : BLK + DEG, :] = degree_ref[0]


def payload_of(total, dense, group, last, degree_rows):
    return pl.pallas_call(
        payload_kernel,
        grid=(REPS,),
        in_specs=[
            pl.BlockSpec((BLK, F), lambda p: (p, 0)),
            pl.BlockSpec((1, BLK, 4 * BLK), lambda p: (group, p, 0)),
            pl.BlockSpec((4 * BLK, F), lambda p: (0, 0)),
            pl.BlockSpec((1, DEG, F), lambda p: (p, 0, 0)),
        ],
        out_specs=pl.BlockSpec((1, BLK + DEG, F), lambda p: (p, 0, 0)),
        out_shape=jax.ShapeDtypeStruct((REPS, BLK + DEG, F), BF),
        compiler_params=pltpu.CompilerParams(vmem_limit_bytes=8 << 20),
        cost_estimate=pl.CostEstimate(
            flops=2 * REPS * BLK * 4 * BLK * F, bytes_accessed=5 << 20, transcendentals=0
        ),
    )(total, dense, last, degree_rows)


def node_kernel(
    got_ref, features_ref, weight_ref, bias_ref, cotangent_ref, act_ref, out_ref
):
    got = got_ref[...].astype(F32)
    summed = jnp.sum(got, axis=0)
    parts = summed[BLK : BLK + 1, :]
    degree_row = 1.0 + parts[:, 0:BLK] + parts[:, BLK : 2 * BLK]
    degree = jnp.transpose(jnp.broadcast_to(degree_row, (BLK, BLK)))
    degree = jnp.concatenate([degree] * 4, axis=1)
    aggregate = summed[0:BLK] + features_ref[...].astype(F32)
    hidden_wide = (aggregate / degree).astype(BF)
    weight = weight_ref[...]
    preact = jnp.dot(hidden_wide, weight, preferred_element_type=F32) + bias_ref[...]
    gate = jax.nn.sigmoid(preact)
    act_ref[...] = (preact * gate).astype(BF)
    slope = (cotangent_ref[...].astype(F32) * gate * (1.0 + preact * (1.0 - gate))).astype(BF)
    rows = lax.dot_general(slope, weight, (((1,), (1,)), ((), ())), preferred_element_type=F32)
    scaled = (rows / degree).astype(BF)
    scaled_t = jnp.transpose(scaled.astype(F32)).astype(BF)
    hidden_t = jnp.transpose(hidden_wide.astype(F32)).astype(BF)
    grad = jnp.dot(hidden_t, slope, preferred_element_type=F32).astype(BF)
    bias = jnp.sum(slope.astype(F32), axis=0, keepdims=True).astype(BF)
    out_ref[:, 768:ROWS, :] = jnp.zeros((REPS, 32, BLK), BF)
    for peer in range(REPS):
        out_ref[peer, 0:512, :] = scaled_t
        for b in range(4):
            out_ref[peer, 512 + 64 * b : 576 + 64 * b, :] = grad[
                64 * peer : 64 * peer + 64, BLK * b : BLK * (b + 1)
            ]
            out_ref[peer, 768 + b : 769 + b, :] = bias[:, BLK * b : BLK * (b + 1)]


def node_step(got, features, weight, bias_row, cotangent):
    return pl.pallas_call(
        node_kernel,
        out_shape=[
            jax.ShapeDtypeStruct((BLK, F), BF),
            jax.ShapeDtypeStruct((REPS, ROWS, BLK), BF),
        ],
        compiler_params=pltpu.CompilerParams(vmem_limit_bytes=24 << 20),
        cost_estimate=pl.CostEstimate(
            flops=6 * BLK * F * F, bytes_accessed=4 << 20, transcendentals=BLK * F
        ),
    )(got, features, weight, bias_row.reshape(1, F), cotangent)


def sum_round(grads, c, *earlier):
    own = after(grads.astype(BF), *earlier)
    return send(own, OUT1), send(own, OUT2)


def sum_rest(grads, first, second, c, *earlier):
    second = after(second, *earlier)
    third = send(second, OUT1)
    fourth = send(lax.dynamic_slice_in_dim(second, c * HALF, HALF, 0), OUT2)
    line = first.astype(F32) + second.astype(F32) + third.astype(F32)
    fourth = lax.dynamic_update_slice_in_dim(
        jnp.zeros((2 * HALF, BLK), F32), fourth.astype(F32), c * HALF, 0
    )
    line = line + fourth
    return grads + line + send(line, CORE)


def product_kernel(groups, first, left_ref, dense_ref, *rest):
    step = pl.program_id(0)
    if first:
        wide_ref = rest[-1]

        @pl.when(step == 0)
        def _():
            for p in range(REPS):
                wide_ref[:, BLK * p : BLK * (p + 1)] = left_ref[p]
    else:
        wide_ref = left_ref
    whole = jnp.dot(wide_ref[...], dense_ref[0], preferred_element_type=F32)
    outs = list(rest)
    for index, group in enumerate(groups):
        if group in (0, 7):
            mine, away = outs.pop(0), outs.pop(0)

            @pl.when(step == index)
            def _():
                if group == 7:
                    mine[...] = whole[:, : 2 * BLK]
                    away[...] = whole[:, 2 * BLK :].astype(BF)
                else:
                    for part in (0, 1):
                        own = 2 * part * BLK
                        here = slice(part * BLK, (part + 1) * BLK)
                        mine[:, here] = whole[:, own : own + BLK]
                        away[:, here] = whole[:, own + BLK : own + 2 * BLK].astype(BF)
        else:
            out = outs.pop(0)

            @pl.when(step == index)
            def _():
                out[...] = whole.astype(out.dtype)


def products(left, dense, groups, first):
    shapes = []
    for group in groups:
        if group in (0, 7):
            shapes += [((F, 2 * BLK), F32), ((F, 2 * BLK), BF)]
        else:
            shapes.append(((F, 4 * BLK), F32 if group % 2 else BF))
    if first:
        shapes.append(((F, REPS * BLK), BF))
        left_spec = pl.BlockSpec((REPS, F, BLK), lambda i: (0, 0, 0))
    else:
        left_spec = pl.BlockSpec((F, REPS * BLK), lambda i: (0, 0))
    top = groups[0]
    return pl.pallas_call(
        functools.partial(product_kernel, groups, first),
        grid=(len(groups),),
        in_specs=[
            left_spec,
            pl.BlockSpec((1, REPS * BLK, 4 * BLK), lambda i: (top - i, 0, 0)),
        ],
        out_specs=[pl.BlockSpec(shape, lambda i: (0, 0)) for shape, _ in shapes],
        out_shape=[jax.ShapeDtypeStruct(shape, dtype) for shape, dtype in shapes],
        compiler_params=pltpu.CompilerParams(vmem_limit_bytes=20 << 20),
        cost_estimate=pl.CostEstimate(
            flops=len(groups) * 2 * F * REPS * BLK * 4 * BLK,
            bytes_accessed=len(groups) * (5 << 19),
            transcendentals=0,
        ),
    )(left, dense)


def forward(features, dense, degree_rows):
    def dot(g, piece):
        return jnp.dot(dense[g], piece, preferred_element_type=F32)

    beside = send(features, SIDE)
    chain = jnp.concatenate([features, send(features, CORE)], axis=0)
    second = send(chain, OUT2)
    own = jnp.concatenate([chain, beside, send(beside, CORE)], axis=0)
    first = send(own, OUT1)
    third = send(second, OUT1)
    fourth = send(second[:BLK], OUT2)
    both2 = jnp.concatenate([second, send(second, SIDE)], axis=0)
    cross2 = send(both2, CORE)
    cross1 = send(first, CORE)
    both3 = jnp.concatenate([third, send(third, SIDE)], axis=0)
    both4 = jnp.concatenate([fourth, send(fourth, SIDE)], axis=0)
    total = dot(0, own) + dot(1, first) + dot(3, both2)
    both3 = after(both3, total)
    cross3 = send(both3, CORE)
    total = total + dot(4, cross2) + dot(2, cross1) + dot(5, both3)
    both4 = after(both4, total)
    last = jnp.concatenate([both4, send(both4, CORE)], axis=0)
    total = total + dot(6, cross3)
    return payload_of(total, dense, 7, last, degree_rows)


def final_kernel(mine_ref, far_ref, near_ref, other_ref, scaled_ref, out_ref):
    total = (
        mine_ref[...]
        + far_ref[:, :BLK].astype(F32)
        + near_ref[:, :BLK].astype(F32)
        + other_ref[...].astype(F32)
        + scaled_ref[0, :F].astype(F32)
    )
    out_ref[...] = jnp.transpose(total).astype(BF)


def final_step(mine, far, near, other, outgoing):
    return pl.pallas_call(
        final_kernel,
        grid=(1,),
        in_specs=[
            pl.BlockSpec((F, BLK), lambda i: (0, 0)),
            pl.BlockSpec((F, 2 * BLK), lambda i: (0, 0)),
            pl.BlockSpec((F, 2 * BLK), lambda i: (0, 0)),
            pl.BlockSpec((F, BLK), lambda i: (0, 0)),
            pl.BlockSpec((1, F, BLK), lambda i: (0, 0, 0)),
        ],
        out_specs=pl.BlockSpec((BLK, F), lambda i: (0, 0)),
        out_shape=jax.ShapeDtypeStruct((BLK, F), BF),
        compiler_params=pltpu.CompilerParams(vmem_limit_bytes=8 << 20),
        cost_estimate=pl.CostEstimate(flops=1 << 19, bytes_accessed=1 << 20, transcendentals=0),
    )(mine, far, near, other, outgoing)


def gradient_kernel(pieces_ref, out_ref):
    for peer in range(REPS):
        for b in range(4):
            out_ref[64 * peer : 64 * peer + 64, BLK * b : BLK * (b + 1)] = pieces_ref[
                peer, 64 * b : 64 * b + 64
            ].astype(F32)


def gradient_of(pieces):
    return pl.pallas_call(
        gradient_kernel,
        out_shape=jax.ShapeDtypeStruct((F, F), F32),
        compiler_params=pltpu.CompilerParams(vmem_limit_bytes=8 << 20),
        cost_estimate=pl.CostEstimate(flops=1 << 18, bytes_accessed=3 << 19, transcendentals=0),
    )(pieces)


def backward(outgoing, everyone, dense, c):
    def over_core(mine, away):
        return mine + send(away, CORE).astype(F32)

    def cut(line):
        width = line.shape[1] // 2
        return line[:, :width], line[:, width:].astype(BF)

    grads = jnp.sum(everyone[:, F:].astype(F32), axis=0)
    grads = grads + send(grads.astype(BF), CORE).astype(F32)
    mine4, away4, away3, mine3, wide = products(everyone, dense, (7, 6, 5), True)
    grads = grads + send(grads.astype(BF), SIDE).astype(F32)
    line4, side4 = cut(over_core(mine4, away4))
    away2, mine2 = products(wide, dense, (4, 3), False)
    line3, side3 = cut(over_core(mine3, away3))
    wide = after(wide, side3, side4)
    away1, mine1, mine0, away0 = products(wide, dense, (2, 1, 0), False)
    grad1, grad2 = sum_round(grads, c, side3, side4)
    line2, side2 = cut(over_core(mine2, away2))
    quad4 = line4 + send(side4, SIDE).astype(F32)
    quad3 = line3 + send(side3, SIDE).astype(F32)
    line1, side1 = cut(over_core(mine1, away1))
    line0, side0 = cut(over_core(mine0, away0))
    away4 = quad4.astype(BF)
    away3 = quad3.astype(BF)
    grads = sum_rest(grads, grad1, grad2, c, away4, away3)
    came4 = send(away4, BACK2).astype(F32)
    came3 = send(away3, BACK1).astype(F32)
    quad2 = line2 + send(side2, SIDE).astype(F32) + came3
    quad1 = line1 + send(side1, SIDE).astype(F32)
    quad0 = line0 + send(side0, SIDE).astype(F32)
    quad2 = jnp.concatenate([quad2[:, :BLK] + came4, quad2[:, BLK:]], axis=1)
    near = send(quad1.astype(BF), BACK1)
    far = send(quad2.astype(BF), BACK2)
    other = send((near[:, BLK:].astype(F32) + far[:, BLK:].astype(F32)).astype(BF), CORE)
    return final_step(quad0, far, near, other, outgoing), grads


def per_device(features, block_columns, block_values, weight, bias_row, cotangent):
    layer = lax.axis_index("layer")
    z, y, c = layer // 4, (layer // 2) % 2, layer % 2
    owner = jnp.where(block_columns >= 0, block_columns, 0) // REPS
    dz = (owner // 4 - z + Z) % Z
    dy = ((owner // 2) % 2 - y) % 2
    dc = (owner % 2 - c) % 2
    near = jnp.where(dz <= 4, dz, Z - dz)
    other = ((dz > 4) != (c == 0)).astype(jnp.int32)
    ends = (near == 0) | (near == 4)
    group = jnp.where(near == 0, 0, jnp.where(near == 4, 7, 2 * near - 1 + other))
    column = jnp.where(near == 4, 2 * dc + dy, 2 * dy + jnp.where(ends, dc, dc ^ other))
    place = jnp.where(block_columns >= 0, 4 * group + column, -1).astype(jnp.int32)
    dense, degree_rows = spread_blocks(place, block_values)
    payload = forward(features, dense, degree_rows)
    got = lax.all_to_all(payload, "rep", 0, 0, tiled=True)

    activations, outgoing = node_step(got, features, weight, bias_row, cotangent)
    everyone = lax.all_to_all(outgoing, "rep", 0, 0, tiled=True)
    feature_grad, grads = backward(outgoing, everyone, dense, c)
    bias_grad = grads[256:260].reshape(F)
    mine = jnp.broadcast_to(grads[:256].astype(BF)[None], (REPS, 256, BLK))
    pieces = lax.all_to_all(mine, "rep", 0, 0, tiled=True)
    weight_grad = gradient_of(pieces)
    return (activations, weight_grad, bias_grad, feature_grad)


def solution(mesh):
    in_specs = (
        P(("layer", "rep"), None),
        P("layer", "rep"),
        P("layer", "rep", None, None),
        P(),
        P(),
        P(("layer", "rep"), None),
    )
    out_specs = (P(("layer", "rep"), None), P(), P(), P(("layer", "rep"), None))
    return jax.shard_map(
        per_device, mesh=mesh, in_specs=in_specs, out_specs=out_specs, check_vma=False
    )
```

```python
import functools

import jax
import jax.numpy as jnp
from jax import lax
from jax.experimental import pallas as pl
from jax.experimental.pallas import tpu as pltpu
from jax.sharding import PartitionSpec as P

BF = jnp.bfloat16
F32 = jnp.float32
Z, Y, C = 8, 2, 2
REPS = 8
BLK = 128
SLOTS = 16
F = 512
GROUPS = 8
DEG = 16
ROWS = 800
HALF = 144
PART = 8


def layer_perm(dz, dy, dc):
    pairs = []
    for z in range(Z):
        for y in range(Y):
            for c in range(C):
                to = (((z + dz) % Z) * Y + (y + dy) % Y) * C + (c + dc) % C
                pairs.append(((z * Y + y) * C + c, to))
    return pairs


def core_perm(hops):
    pairs = []
    for z in range(Z):
        for y in range(Y):
            for c in range(C):
                step = hops if c == 0 else -hops
                pairs.append(((z * Y + y) * C + c, (((z + step) % Z) * Y + y) * C + c))
    return pairs


OUT1, OUT2 = core_perm(1), core_perm(2)
BACK1, BACK2 = core_perm(-1), core_perm(-2)
SIDE = layer_perm(0, 1, 0)
CORE = layer_perm(0, 0, 1)

def send(value, perm):
    return lax.ppermute(value, "layer", perm)


def after(value, *earlier):
    return lax.optimization_barrier((value,) + earlier)[0]


def spread_kernel(first, place_ref, values_ref, *rest):
    dense_ref, degree_ref, tiles, sems = rest[-4:]
    step = pl.program_id(0)

    def fetch(p):
        return pltpu.make_async_copy(values_ref.at[first + p], tiles.at[p], sems.at[p])

    @pl.when(step == 0)
    def _():
        for p in range(PART):
            fetch(p).start()

    dense_ref[...] = jnp.zeros_like(dense_ref)
    fetch(step).wait()
    total = jnp.zeros((BLK, BLK), jnp.int32)
    for slot in reversed(range(SLOTS)):
        tile = tiles[step, slot]
        total = total + tile
        place = place_ref[(first + step) * SLOTS + slot]
        lane = pl.multiple_of((place % 4) * BLK, BLK)
        dense_ref[place // 4, :, pl.ds(lane, BLK)] = tile.astype(F32).astype(BF)

    row = lax.dot_general(
        jnp.ones((DEG, BLK), BF),
        total.astype(F32).astype(BF),
        (((1,), (1,)), ((), ())),
        preferred_element_type=F32,
    )
    high = jnp.floor(row * (1.0 / 128.0)) * 128.0
    degree_ref[...] = jnp.zeros_like(degree_ref)
    degree_ref[0, :, 0:BLK] = high.astype(BF)
    degree_ref[0, :, BLK : 2 * BLK] = (row - high).astype(BF)


def spread_part(place, values, first, dense=None):
    panels = values.shape[0]
    given = [] if dense is None else [dense]
    return pl.pallas_call(
        functools.partial(spread_kernel, first),
        grid_spec=pltpu.PrefetchScalarGridSpec(
            num_scalar_prefetch=1,
            grid=(PART,),
            in_specs=[pl.BlockSpec(memory_space=pltpu.HBM)]
            + [pl.BlockSpec(memory_space=pl.ANY)] * len(given),
            out_specs=[
                pl.BlockSpec((GROUPS, BLK, 4 * BLK), lambda p, place: (0, first + p, 0)),
                pl.BlockSpec((1, DEG, F), lambda p, place: (p, 0, 0)),
            ],
            scratch_shapes=[
                pltpu.VMEM((PART, SLOTS, BLK, BLK), jnp.int32),
                pltpu.SemaphoreType.DMA((PART,)),
            ],
        ),
        out_shape=[
            jax.ShapeDtypeStruct((GROUPS, panels * BLK, 4 * BLK), BF),
            jax.ShapeDtypeStruct((PART, DEG, F), BF),
        ],
        input_output_aliases={2: 0} if given else {},
        compiler_params=pltpu.CompilerParams(vmem_limit_bytes=16 << 20),
        cost_estimate=pl.CostEstimate(flops=1 << 21, bytes_accessed=8 << 20, transcendentals=0),
    )(place.reshape(-1), pltpu.with_memory_space_constraint(values, pltpu.HBM), *given)


def payload_kernel(total_ref, dense_ref, last_ref, degree_ref, out_ref):
    product = jnp.dot(dense_ref[0], last_ref[...], preferred_element_type=F32)
    out_ref[0, 0:BLK, :] = (total_ref[...] + product).astype(BF)
    out_ref[0, BLK : BLK + DEG, :] = degree_ref[0]


def payload_of(total, dense, group, last, degree_rows):
    return pl.pallas_call(
        payload_kernel,
        grid=(REPS,),
        in_specs=[
            pl.BlockSpec((BLK, F), lambda p: (p, 0)),
            pl.BlockSpec((1, BLK, 4 * BLK), lambda p: (group, p, 0)),
            pl.BlockSpec((4 * BLK, F), lambda p: (0, 0)),
            pl.BlockSpec((1, DEG, F), lambda p: (p, 0, 0)),
        ],
        out_specs=pl.BlockSpec((1, BLK + DEG, F), lambda p: (p, 0, 0)),
        out_shape=jax.ShapeDtypeStruct((REPS, BLK + DEG, F), BF),
        compiler_params=pltpu.CompilerParams(vmem_limit_bytes=8 << 20),
        cost_estimate=pl.CostEstimate(
            flops=2 * REPS * BLK * 4 * BLK * F, bytes_accessed=5 << 20, transcendentals=0
        ),
    )(total, dense, last, degree_rows)


def node_kernel(
    got_ref, features_ref, weight_ref, bias_ref, cotangent_ref, act_ref, out_ref, scaled_ref
):
    got = got_ref[...].astype(F32)
    summed = jnp.sum(got, axis=0)
    parts = summed[BLK : BLK + 1, :]
    degree_row = 1.0 + parts[:, 0:BLK] + parts[:, BLK : 2 * BLK]
    degree = jnp.transpose(jnp.broadcast_to(degree_row, (BLK, BLK)))
    degree = jnp.concatenate([degree] * 4, axis=1)
    aggregate = summed[0:BLK] + features_ref[...].astype(F32)
    hidden_wide = (aggregate / degree).astype(BF)
    weight = weight_ref[...]
    preact = jnp.dot(hidden_wide, weight, preferred_element_type=F32) + bias_ref[...]
    gate = jax.nn.sigmoid(preact)
    act_ref[...] = (preact * gate).astype(BF)
    slope = (cotangent_ref[...].astype(F32) * gate * (1.0 + preact * (1.0 - gate))).astype(BF)
    rows = lax.dot_general(slope, weight, (((1,), (1,)), ((), ())), preferred_element_type=F32)
    scaled = (rows / degree).astype(BF)
    scaled_t = jnp.transpose(scaled.astype(F32)).astype(BF)
    scaled_ref[...] = scaled_t
    hidden_t = jnp.transpose(hidden_wide.astype(F32)).astype(BF)
    grad = jnp.dot(hidden_t, slope, preferred_element_type=F32).astype(BF)
    bias = jnp.sum(slope.astype(F32), axis=0, keepdims=True).astype(BF)
    out_ref[:, 768:ROWS, :] = jnp.zeros((REPS, 32, BLK), BF)
    for peer in range(REPS):
        out_ref[peer, 0:512, :] = scaled_t
        for b in range(4):
            out_ref[peer, 512 + 64 * b : 576 + 64 * b, :] = grad[
                64 * peer : 64 * peer + 64, BLK * b : BLK * (b + 1)
            ]
            out_ref[peer, 768 + b : 769 + b, :] = bias[:, BLK * b : BLK * (b + 1)]


def node_step(got, features, weight, bias_row, cotangent):
    return pl.pallas_call(
        node_kernel,
        out_shape=[
            jax.ShapeDtypeStruct((BLK, F), BF),
            jax.ShapeDtypeStruct((REPS, ROWS, BLK), BF),
            jax.ShapeDtypeStruct((F, BLK), BF),
        ],
        compiler_params=pltpu.CompilerParams(vmem_limit_bytes=24 << 20),
        cost_estimate=pl.CostEstimate(
            flops=6 * BLK * F * F, bytes_accessed=4 << 20, transcendentals=BLK * F
        ),
    )(got, features, weight, bias_row.reshape(1, F), cotangent)


def product_kernel(groups, first, left_ref, dense_ref, *rest):
    step = pl.program_id(0)
    if first:
        wide_ref = rest[-1]

        @pl.when(step == 0)
        def _():
            for p in range(REPS):
                wide_ref[:, BLK * p : BLK * (p + 1)] = left_ref[p]
    else:
        wide_ref = left_ref
    whole = jnp.dot(wide_ref[...], dense_ref[0], preferred_element_type=F32)
    away_ref, mine_ref = rest[:2]
    for index, group in enumerate(groups):

        @pl.when(step == index)
        def _():
            if group == 7:
                away_ref[:, : 2 * BLK] = whole[:, 2 * BLK :].astype(BF)
                mine_ref[:, : 2 * BLK] = whole[:, : 2 * BLK]
            elif group == 0:
                for part in (0, 1):
                    own = 2 * part * BLK
                    here = slice(part * BLK, (part + 1) * BLK)
                    rest[2][:, here] = whole[:, own + BLK : own + 2 * BLK].astype(BF)
                    rest[3][:, here] = whole[:, own : own + BLK]
            elif group % 2:
                mine_ref[:, mine_ref.shape[1] - 4 * BLK :] = whole
            else:
                away_ref[:, away_ref.shape[1] - 4 * BLK :] = whole.astype(BF)


def products(left, dense, groups, first):
    columns = 6 * BLK if 7 in groups else 4 * BLK
    shapes = [((F, columns), BF), ((F, columns), F32)]
    if 0 in groups:
        shapes += [((F, 2 * BLK), BF), ((F, 2 * BLK), F32)]
    if first:
        shapes.append(((F, REPS * BLK), BF))
        left_spec = pl.BlockSpec((REPS, F, BLK), lambda i: (0, 0, 0))
    else:
        left_spec = pl.BlockSpec((F, REPS * BLK), lambda i: (0, 0))
    top = groups[0]
    return pl.pallas_call(
        functools.partial(product_kernel, groups, first),
        grid=(len(groups),),
        in_specs=[
            left_spec,
            pl.BlockSpec((1, REPS * BLK, 4 * BLK), lambda i: (top - i, 0, 0)),
        ],
        out_specs=[pl.BlockSpec(shape, lambda i: (0, 0)) for shape, _ in shapes],
        out_shape=[jax.ShapeDtypeStruct(shape, dtype) for shape, dtype in shapes],
        compiler_params=pltpu.CompilerParams(vmem_limit_bytes=20 << 20),
        cost_estimate=pl.CostEstimate(
            flops=len(groups) * 2 * F * REPS * BLK * 4 * BLK,
            bytes_accessed=len(groups) * (5 << 19),
            transcendentals=0,
        ),
    )(left, dense)


def forward(features, place, values):
    def dot(g, piece):
        return jnp.dot(dense[g], piece, preferred_element_type=F32)

    chain = jnp.concatenate([features, send(features, CORE)], axis=0)
    beside = send(features, SIDE)
    second = send(chain, OUT2)
    own = jnp.concatenate([chain, beside, send(beside, CORE)], axis=0)
    first = send(own, OUT1)
    dense, degree_rows = spread_part(after(place, own), values, 0)
    third = send(second, OUT1)
    fourth = send(second[:BLK], OUT2)
    both2 = jnp.concatenate([second, send(second, SIDE)], axis=0)
    cross2 = send(both2, CORE)
    cross1 = send(first, CORE)
    both3 = jnp.concatenate([third, send(third, SIDE)], axis=0)
    both4 = jnp.concatenate([fourth, send(fourth, SIDE)], axis=0)
    total = dot(0, own) + dot(1, first) + dot(3, both2)
    both3 = after(both3, total)
    cross3 = send(both3, CORE)
    total = total + dot(4, cross2) + dot(2, cross1) + dot(5, both3)
    both4 = after(both4, total)
    last = jnp.concatenate([both4, send(both4, CORE)], axis=0)
    total = total + dot(6, cross3)
    return payload_of(total, dense, 7, last, degree_rows), dense


def final_kernel(mine_ref, far_ref, near_ref, other_ref, scaled_ref, out_ref):
    total = (
        mine_ref[...]
        + far_ref[:, :BLK].astype(F32)
        + near_ref[:, :BLK].astype(F32)
        + other_ref[...].astype(F32)
        + scaled_ref[...].astype(F32)
    )
    out_ref[...] = jnp.transpose(total).astype(BF)


def final_step(*parts):
    return pl.pallas_call(
        final_kernel,
        out_shape=jax.ShapeDtypeStruct((BLK, F), BF),
        compiler_params=pltpu.CompilerParams(vmem_limit_bytes=8 << 20),
        cost_estimate=pl.CostEstimate(flops=1 << 19, bytes_accessed=1 << 20, transcendentals=0),
    )(*parts)


def gradient_kernel(pieces_ref, out_ref):
    for peer in range(REPS):
        for b in range(4):
            out_ref[64 * peer : 64 * peer + 64, BLK * b : BLK * (b + 1)] = pieces_ref[
                peer, 64 * b : 64 * b + 64
            ].astype(F32)


def gradient_of(pieces):
    return pl.pallas_call(
        gradient_kernel,
        out_shape=jax.ShapeDtypeStruct((F, F), F32),
        compiler_params=pltpu.CompilerParams(vmem_limit_bytes=8 << 20),
        cost_estimate=pl.CostEstimate(flops=1 << 18, bytes_accessed=3 << 19, transcendentals=0),
    )(pieces)


def folded(rows):
    half = rows.shape[0] // 2
    return jnp.concatenate([rows[:half], rows[half:]], axis=1)


def unfolded(rows):
    return jnp.concatenate([rows[:, :BLK], rows[:, BLK:]], axis=0)


def backward(everyone, dense, scaled_t):
    def wide_of(value):
        return value.astype(F32)

    def stacked(*parts):
        return jnp.concatenate([part.astype(BF) for part in parts], axis=0)

    grads = jnp.sum(wide_of(everyone[:, F:]), axis=0)
    grads = folded(grads + wide_of(send(grads.astype(BF), CORE)))
    away, mine, wide = products(everyone, dense, (7, 6, 5), True)
    line = mine + wide_of(send(away, CORE))
    side3 = stacked(line[:, 4 * BLK :], grads)
    got3 = wide_of(send(side3, SIDE))
    side4 = line[:, BLK : 2 * BLK].astype(BF)
    got4 = wide_of(send(side4, SIDE))
    away, mine = products(wide, dense, (4, 3), False)
    line2 = mine + wide_of(after(send(away, CORE), side3, side4))
    side2 = line2[:, 2 * BLK :].astype(BF)
    got2 = wide_of(send(side2, SIDE))
    away1, mine1, away0, mine0 = products(after(wide, side3, side4), dense, (2, 1, 0), False)
    line1 = mine1 + wide_of(send(away1, CORE))
    side1 = after(line1[:, 2 * BLK :].astype(BF), side2)
    got1 = wide_of(send(side1, SIDE))
    line0 = mine0 + wide_of(send(away0, CORE))
    side0 = after(line0[:, BLK:].astype(BF), side1)
    quad0 = line0[:, :BLK] + wide_of(send(side0, SIDE))

    grads = grads + got3[F:]
    quad3 = after(stacked(line[:, 2 * BLK : 4 * BLK] + got3[:F], grads), side1)
    quad4 = after(stacked(line[:, :BLK] + got4, unfolded(grads)), side1)
    came3 = send(quad3, BACK1)
    came4 = send(quad4, BACK2)
    quad2 = line2[:, : 2 * BLK] + got2 + wide_of(came3[:F])
    quad2 = jnp.concatenate([quad2[:, :BLK] + wide_of(came4[:F]), quad2[:, BLK:]], axis=1)
    quad2 = quad2.astype(BF)
    far = send(quad2, BACK2)
    quad1 = (line1[:, : 2 * BLK] + got1).astype(BF)
    near = send(quad1, BACK1)

    both = jnp.concatenate([came3[F:], folded(came4[F:])], axis=0)
    more = wide_of(send(after(both, quad2), BACK2))
    rows = both.shape[0] // 2
    around = wide_of(both[:rows]) + wide_of(both[rows:]) + more[:rows] + 0.5 * more[rows:]
    grads = after(grads + around + send(around, CORE), quad1)

    other = send((wide_of(far[:, BLK:]) + wide_of(near[:, BLK:])).astype(BF), CORE)
    return final_step(quad0, far, near, other, scaled_t), unfolded(grads)


def per_device(features, block_columns, block_values, weight, bias_row, cotangent):
    layer = lax.axis_index("layer")
    z, y, c = layer // 4, (layer // 2) % 2, layer % 2
    owner = jnp.where(block_columns >= 0, block_columns, 0) // REPS
    dz = (owner // 4 - z + Z) % Z
    dy = ((owner // 2) % 2 - y) % 2
    dc = (owner % 2 - c) % 2
    near = jnp.where(dz <= 4, dz, Z - dz)
    other = ((dz > 4) != (c == 0)).astype(jnp.int32)
    ends = (near == 0) | (near == 4)
    group = jnp.where(near == 0, 0, jnp.where(near == 4, 7, 2 * near - 1 + other))
    column = jnp.where(near == 4, 2 * dc + dy, 2 * dy + jnp.where(ends, dc, dc ^ other))
    place = 4 * group + column
    place = jnp.where(block_columns >= 0, place, place[:, 0:1]).astype(jnp.int32)
    payload, dense = forward(features, place, block_values)
    got = lax.all_to_all(payload, "rep", 0, 0, tiled=True)

    activations, outgoing, scaled_t = node_step(got, features, weight, bias_row, cotangent)
    everyone = lax.all_to_all(outgoing, "rep", 0, 0, tiled=True)
    feature_grad, grads = backward(everyone, dense, scaled_t)
    bias_grad = grads[256:260].reshape(F)
    mine = jnp.broadcast_to(grads[:256].astype(BF)[None], (REPS, 256, BLK))
    pieces = lax.all_to_all(mine, "rep", 0, 0, tiled=True)
    weight_grad = gradient_of(pieces)
    return (activations, weight_grad, bias_grad, feature_grad)


def solution(mesh):
    in_specs = (
        P(("layer", "rep"), None),
        P("layer", "rep"),
        P("layer", "rep", None, None),
        P(),
        P(),
        P(("layer", "rep"), None),
    )
    out_specs = (P(("layer", "rep"), None), P(), P(), P(("layer", "rep"), None))
    return jax.shard_map(
        per_device, mesh=mesh, in_specs=in_specs, out_specs=out_specs, check_vma=False
    )
```

```python
import functools

import jax
import jax.numpy as jnp
from jax import lax
from jax.experimental import pallas as pl
from jax.experimental.pallas import tpu as pltpu
from jax.sharding import PartitionSpec as P

BF = jnp.bfloat16
F32 = jnp.float32
Z, Y, C = 8, 2, 2
REPS = 8
BLK = 128
SLOTS = 16
F = 512
GROUPS = 8
DEG = 16
ROWS = 800
HALF = 144
PART = 8


def layer_perm(dz, dy, dc):
    pairs = []
    for z in range(Z):
        for y in range(Y):
            for c in range(C):
                to = (((z + dz) % Z) * Y + (y + dy) % Y) * C + (c + dc) % C
                pairs.append(((z * Y + y) * C + c, to))
    return pairs


def core_perm(hops):
    pairs = []
    for z in range(Z):
        for y in range(Y):
            for c in range(C):
                step = hops if c == 0 else -hops
                pairs.append(((z * Y + y) * C + c, (((z + step) % Z) * Y + y) * C + c))
    return pairs


OUT1, OUT2 = core_perm(1), core_perm(2)
BACK1, BACK2, BACK3, BACK4 = (core_perm(-hops) for hops in (1, 2, 3, 4))
SIDE = layer_perm(0, 1, 0)
CORE = layer_perm(0, 0, 1)

def send(value, perm):
    return lax.ppermute(value, "layer", perm)


def after(value, *earlier):
    return lax.optimization_barrier((value,) + earlier)[0]


def spread_kernel(first, place_ref, values_ref, *rest):
    dense_ref, degree_ref, tiles, sems = rest[-4:]
    step = pl.program_id(0)

    def fetch(p):
        return pltpu.make_async_copy(values_ref.at[first + p], tiles.at[p], sems.at[p])

    @pl.when(step == 0)
    def _():
        for p in range(PART):
            fetch(p).start()

    dense_ref[...] = jnp.zeros_like(dense_ref)
    fetch(step).wait()
    total = jnp.zeros((BLK, BLK), jnp.int32)
    for slot in reversed(range(SLOTS)):
        tile = tiles[step, slot]
        total = total + tile
        place = place_ref[(first + step) * SLOTS + slot]
        lane = pl.multiple_of((place % 4) * BLK, BLK)
        dense_ref[place // 4, :, pl.ds(lane, BLK)] = tile.astype(F32).astype(BF)

    row = lax.dot_general(
        jnp.ones((DEG, BLK), BF),
        total.astype(F32).astype(BF),
        (((1,), (1,)), ((), ())),
        preferred_element_type=F32,
    )
    high = jnp.floor(row * (1.0 / 128.0)) * 128.0
    degree_ref[...] = jnp.zeros_like(degree_ref)
    degree_ref[0, :, 0:BLK] = high.astype(BF)
    degree_ref[0, :, BLK : 2 * BLK] = (row - high).astype(BF)


def spread_part(place, values, first, dense=None):
    panels = values.shape[0]
    given = [] if dense is None else [dense]
    return pl.pallas_call(
        functools.partial(spread_kernel, first),
        grid_spec=pltpu.PrefetchScalarGridSpec(
            num_scalar_prefetch=1,
            grid=(PART,),
            in_specs=[pl.BlockSpec(memory_space=pltpu.HBM)]
            + [pl.BlockSpec(memory_space=pl.ANY)] * len(given),
            out_specs=[
                pl.BlockSpec((GROUPS, BLK, 4 * BLK), lambda p, place: (0, first + p, 0)),
                pl.BlockSpec((1, DEG, F), lambda p, place: (p, 0, 0)),
            ],
            scratch_shapes=[
                pltpu.VMEM((PART, SLOTS, BLK, BLK), jnp.int32),
                pltpu.SemaphoreType.DMA((PART,)),
            ],
        ),
        out_shape=[
            jax.ShapeDtypeStruct((GROUPS, panels * BLK, 4 * BLK), BF),
            jax.ShapeDtypeStruct((PART, DEG, F), BF),
        ],
        input_output_aliases={2: 0} if given else {},
        compiler_params=pltpu.CompilerParams(vmem_limit_bytes=16 << 20),
        cost_estimate=pl.CostEstimate(flops=1 << 21, bytes_accessed=8 << 20, transcendentals=0),
    )(place.reshape(-1), pltpu.with_memory_space_constraint(values, pltpu.HBM), *given)


def payload_kernel(total_ref, dense_ref, last_ref, degree_ref, out_ref):
    product = jnp.dot(dense_ref[0], last_ref[...], preferred_element_type=F32)
    whole = (total_ref[...] + product).astype(BF)
    for p in range(2):
        out_ref[p, 0:BLK, :] = whole[p * BLK : (p + 1) * BLK]
        out_ref[p, BLK : BLK + DEG, :] = degree_ref[p]


def payload_of(total, dense, group, last, degree_rows):
    return pl.pallas_call(
        payload_kernel,
        grid=(REPS // 2,),
        in_specs=[
            pl.BlockSpec((2 * BLK, F), lambda p: (p, 0)),
            pl.BlockSpec((1, 2 * BLK, 4 * BLK), lambda p: (group, p, 0)),
            pl.BlockSpec((4 * BLK, F), lambda p: (0, 0)),
            pl.BlockSpec((2, DEG, F), lambda p: (p, 0, 0)),
        ],
        out_specs=pl.BlockSpec((2, BLK + DEG, F), lambda p: (p, 0, 0)),
        out_shape=jax.ShapeDtypeStruct((REPS, BLK + DEG, F), BF),
        compiler_params=pltpu.CompilerParams(vmem_limit_bytes=8 << 20),
        cost_estimate=pl.CostEstimate(
            flops=2 * REPS * BLK * 4 * BLK * F, bytes_accessed=5 << 20, transcendentals=0
        ),
    )(total, dense, last, degree_rows)


def node_kernel(
    got_ref, features_ref, weight_ref, bias_ref, cotangent_ref, act_ref, out_ref, scaled_ref
):
    got = got_ref[...].astype(F32)
    summed = jnp.sum(got, axis=0)
    parts = summed[BLK : BLK + 1, :]
    degree_row = 1.0 + parts[:, 0:BLK] + parts[:, BLK : 2 * BLK]
    degree = jnp.transpose(jnp.broadcast_to(degree_row, (BLK, BLK)))
    degree = jnp.concatenate([degree] * 4, axis=1)
    aggregate = summed[0:BLK] + features_ref[...].astype(F32)
    hidden_wide = (aggregate / degree).astype(BF)
    weight = weight_ref[...]
    preact = jnp.dot(hidden_wide, weight, preferred_element_type=F32) + bias_ref[...]
    gate = jax.nn.sigmoid(preact)
    act_ref[...] = (preact * gate).astype(BF)
    slope = (cotangent_ref[...].astype(F32) * gate * (1.0 + preact * (1.0 - gate))).astype(BF)
    rows = lax.dot_general(slope, weight, (((1,), (1,)), ((), ())), preferred_element_type=F32)
    scaled = (rows / degree).astype(BF)
    scaled_t = jnp.transpose(scaled.astype(F32)).astype(BF)
    scaled_ref[...] = scaled_t
    hidden_t = jnp.transpose(hidden_wide.astype(F32)).astype(BF)
    grad = jnp.dot(hidden_t, slope, preferred_element_type=F32).astype(BF)
    bias = jnp.sum(slope.astype(F32), axis=0, keepdims=True).astype(BF)
    out_ref[:, 768:ROWS, :] = jnp.zeros((REPS, 32, BLK), BF)
    for peer in range(REPS):
        out_ref[peer, 0:512, :] = scaled_t
        for b in range(4):
            out_ref[peer, 512 + 64 * b : 576 + 64 * b, :] = grad[
                64 * peer : 64 * peer + 64, BLK * b : BLK * (b + 1)
            ]
            out_ref[peer, 768 + b : 769 + b, :] = bias[:, BLK * b : BLK * (b + 1)]


def node_step(got, features, weight, bias_row, cotangent):
    return pl.pallas_call(
        node_kernel,
        out_shape=[
            jax.ShapeDtypeStruct((BLK, F), BF),
            jax.ShapeDtypeStruct((REPS, ROWS, BLK), BF),
            jax.ShapeDtypeStruct((F, BLK), BF),
        ],
        compiler_params=pltpu.CompilerParams(vmem_limit_bytes=24 << 20),
        cost_estimate=pl.CostEstimate(
            flops=6 * BLK * F * F, bytes_accessed=4 << 20, transcendentals=BLK * F
        ),
    )(got, features, weight, bias_row.reshape(1, F), cotangent)


def product_kernel(groups, first, left_ref, dense_ref, *rest):
    step = pl.program_id(0)
    if first:
        wide_ref = rest[-1]

        @pl.when(step == 0)
        def _():
            for p in range(REPS):
                wide_ref[:, BLK * p : BLK * (p + 1)] = left_ref[p]
    else:
        wide_ref = left_ref
    whole = jnp.dot(wide_ref[...], dense_ref[0], preferred_element_type=F32)
    away_ref, mine_ref = rest[:2]
    for index, group in enumerate(groups):

        @pl.when(step == index)
        def _():
            if group == 7:
                away_ref[:, : 2 * BLK] = whole[:, 2 * BLK :].astype(BF)
                mine_ref[:, : 2 * BLK] = whole[:, : 2 * BLK]
            elif group == 0:
                for part in (0, 1):
                    own = 2 * part * BLK
                    here = slice(part * BLK, (part + 1) * BLK)
                    rest[2][:, here] = whole[:, own + BLK : own + 2 * BLK].astype(BF)
                    rest[3][:, here] = whole[:, own : own + BLK]
            elif group % 2:
                mine_ref[:, mine_ref.shape[1] - 4 * BLK :] = whole
            else:
                away_ref[:, away_ref.shape[1] - 4 * BLK :] = whole.astype(BF)


def products(left, dense, groups, first):
    columns = 6 * BLK if 7 in groups else 4 * BLK
    shapes = [((F, columns), BF), ((F, columns), F32)]
    if 0 in groups:
        shapes += [((F, 2 * BLK), BF), ((F, 2 * BLK), F32)]
    if first:
        shapes.append(((F, REPS * BLK), BF))
        left_spec = pl.BlockSpec((REPS, F, BLK), lambda i: (0, 0, 0))
    else:
        left_spec = pl.BlockSpec((F, REPS * BLK), lambda i: (0, 0))
    top = groups[0]
    return pl.pallas_call(
        functools.partial(product_kernel, groups, first),
        grid=(len(groups),),
        in_specs=[
            left_spec,
            pl.BlockSpec((1, REPS * BLK, 4 * BLK), lambda i: (top - i, 0, 0)),
        ],
        out_specs=[pl.BlockSpec(shape, lambda i: (0, 0)) for shape, _ in shapes],
        out_shape=[jax.ShapeDtypeStruct(shape, dtype) for shape, dtype in shapes],
        compiler_params=pltpu.CompilerParams(vmem_limit_bytes=20 << 20),
        cost_estimate=pl.CostEstimate(
            flops=len(groups) * 2 * F * REPS * BLK * 4 * BLK,
            bytes_accessed=len(groups) * (5 << 19),
            transcendentals=0,
        ),
    )(left, dense)


def forward(features, place_of, values):
    def dot(g, piece):
        return jnp.dot(dense[g], piece, preferred_element_type=F32)

    chain = jnp.concatenate([features, send(features, CORE)], axis=0)
    beside = send(features, SIDE)
    second = send(chain, OUT2)
    place = place_of(chain)
    early = place
    own = jnp.concatenate([chain, beside, send(beside, CORE)], axis=0)
    early = after(early, own)
    dense, degree_rows = spread_part(early, values, 0)
    first = send(own, OUT1)
    third = send(second, OUT1)
    total = dot(0, own)
    fourth = send(second[:BLK], OUT2)
    both2 = jnp.concatenate([second, send(second, SIDE)], axis=0)
    cross2 = send(both2, CORE)
    cross1 = send(first, CORE)
    both3 = jnp.concatenate([third, send(third, SIDE)], axis=0)
    both4 = jnp.concatenate([fourth, send(fourth, SIDE)], axis=0)
    total = total + dot(1, first) + dot(3, both2)
    total = total + dot(4, cross2) + dot(2, cross1)
    both4 = after(both4, total)
    last = jnp.concatenate([both4, send(both4, CORE)], axis=0)
    total = total + dot(7, last)
    both3 = after(both3, total)
    cross3 = send(both3, CORE)
    total = total + dot(5, both3)
    return payload_of(total, dense, 6, cross3, degree_rows), dense


def final_kernel(mine_ref, far_ref, near_ref, other_ref, scaled_ref, out_ref):
    total = (
        mine_ref[...]
        + far_ref[:, :BLK].astype(F32)
        + near_ref[:, :BLK].astype(F32)
        + other_ref[...].astype(F32)
        + scaled_ref[...].astype(F32)
    )
    out_ref[...] = jnp.transpose(total).astype(BF)


def final_step(*parts):
    return pl.pallas_call(
        final_kernel,
        out_shape=jax.ShapeDtypeStruct((BLK, F), BF),
        compiler_params=pltpu.CompilerParams(vmem_limit_bytes=8 << 20),
        cost_estimate=pl.CostEstimate(flops=1 << 19, bytes_accessed=1 << 20, transcendentals=0),
    )(*parts)


def gradient_kernel(pieces_ref, out_ref):
    for peer in range(REPS):
        for b in range(4):
            out_ref[64 * peer : 64 * peer + 64, BLK * b : BLK * (b + 1)] = pieces_ref[
                peer, 64 * b : 64 * b + 64
            ].astype(F32)


def gradient_of(pieces):
    return pl.pallas_call(
        gradient_kernel,
        out_shape=jax.ShapeDtypeStruct((F, F), F32),
        compiler_params=pltpu.CompilerParams(vmem_limit_bytes=8 << 20),
        cost_estimate=pl.CostEstimate(flops=1 << 18, bytes_accessed=3 << 19, transcendentals=0),
    )(pieces)


def folded(rows):
    half = rows.shape[0] // 2
    return jnp.concatenate([rows[:half], rows[half:]], axis=1)


def unfolded(rows):
    return jnp.concatenate([rows[:, :BLK], rows[:, BLK:]], axis=0)


def backward(everyone, dense, scaled_t):
    def wide_of(value):
        return value.astype(F32)

    def stacked(*parts):
        return jnp.concatenate([part.astype(BF) for part in parts], axis=0)

    grads = jnp.sum(wide_of(everyone[:, F:]), axis=0)
    grads = folded(grads + wide_of(send(grads.astype(BF), CORE)))
    away, mine, wide = products(everyone, dense, (7, 6, 5), True)
    line = mine + wide_of(send(away, CORE))
    side3 = stacked(line[:, 4 * BLK :], grads)
    got3 = wide_of(send(side3, SIDE))
    side4 = line[:, BLK : 2 * BLK].astype(BF)
    away, mine = products(wide, dense, (4, 3), False)
    line2 = mine + wide_of(after(send(away, CORE), side3))
    side2 = line2[:, 2 * BLK :].astype(BF)
    got4 = wide_of(send(side4, SIDE))
    got2 = wide_of(send(side2, SIDE))
    away1, mine1, away0, mine0 = products(after(wide, side3), dense, (2, 1, 0), False)
    line1 = mine1 + wide_of(send(away1, CORE))
    side1 = after(line1[:, 2 * BLK :].astype(BF), side2)
    got1 = wide_of(send(side1, SIDE))
    line0 = mine0 + wide_of(send(away0, CORE))
    side0 = after(line0[:, BLK:].astype(BF), side1)
    quad0 = line0[:, :BLK] + wide_of(send(side0, SIDE))

    grads = grads + got3[F:]
    quad3 = stacked(line[:, 2 * BLK : 4 * BLK] + got3[:F], grads)
    quad4 = stacked(line[:, :BLK] + got4, unfolded(grads))
    quad3 = after(quad3, side2)
    quad4 = after(quad4, side2)
    came3 = send(quad3, BACK1)
    came4 = send(quad4, BACK2)
    quad2 = line2[:, : 2 * BLK] + got2 + wide_of(came3[:F])
    quad2 = jnp.concatenate([quad2[:, :BLK] + wide_of(came4[:F]), quad2[:, BLK:]], axis=1)
    quad2 = quad2.astype(BF)
    far = send(quad2, BACK2)
    quad1 = (line1[:, : 2 * BLK] + got1).astype(BF)
    near = send(quad1, BACK1)

    own = grads.astype(BF)
    own = after(own, quad3, quad4)
    third = send(own, BACK3)
    fourth = send(own, BACK4)
    around = wide_of(came3[F:]) + wide_of(folded(came4[F:]))
    around = around + wide_of(third) + 0.5 * wide_of(fourth)
    got = send(around, CORE)
    got = after(got, quad2)
    grads = grads + around + got

    other = send((wide_of(far[:, BLK:]) + wide_of(near[:, BLK:])).astype(BF), CORE)
    return final_step(quad0, far, near, other, scaled_t), unfolded(grads)


def per_device(features, block_columns, block_values, weight, bias_row, cotangent):
    def place_of(chain):
        layer = lax.axis_index("layer")
        z, y, c = layer // 4, (layer // 2) % 2, layer % 2
        columns = after(block_columns, chain)
        owner = jnp.where(columns >= 0, columns, 0) // REPS
        dz = (owner // 4 - z + Z) % Z
        dy = ((owner // 2) % 2 - y) % 2
        dc = (owner % 2 - c) % 2
        near = jnp.where(dz <= 4, dz, Z - dz)
        other = ((dz > 4) != (c == 0)).astype(jnp.int32)
        ends = (near == 0) | (near == 4)
        group = jnp.where(near == 0, 0, jnp.where(near == 4, 7, 2 * near - 1 + other))
        column = jnp.where(near == 4, 2 * dc + dy, 2 * dy + jnp.where(ends, dc, dc ^ other))
        place = 4 * group + column
        return jnp.where(columns >= 0, place, place[:, 0:1]).astype(jnp.int32)

    payload, dense = forward(features, place_of, block_values)
    got = lax.all_to_all(payload, "rep", 0, 0, tiled=True)

    activations, outgoing, scaled_t = node_step(got, features, weight, bias_row, cotangent)
    everyone = lax.all_to_all(outgoing, "rep", 0, 0, tiled=True)
    feature_grad, grads = backward(everyone, dense, scaled_t)
    bias_grad = grads[256:260].reshape(F)
    mine = jnp.broadcast_to(grads[:256].astype(BF)[None], (REPS, 256, BLK))
    pieces = lax.all_to_all(mine, "rep", 0, 0, tiled=True)
    weight_grad = gradient_of(pieces)
    return (activations, weight_grad, bias_grad, feature_grad)


def solution(mesh):
    in_specs = (
        P(("layer", "rep"), None),
        P("layer", "rep"),
        P("layer", "rep", None, None),
        P(),
        P(),
        P(("layer", "rep"), None),
    )
    out_specs = (P(("layer", "rep"), None), P(), P(), P(("layer", "rep"), None))
    return jax.shard_map(
        per_device, mesh=mesh, in_specs=in_specs, out_specs=out_specs, check_vma=False
    )
```

```python
import functools

import jax
import jax.numpy as jnp
from jax import lax
from jax.experimental import pallas as pl
from jax.experimental.pallas import tpu as pltpu
from jax.sharding import PartitionSpec as P

BF = jnp.bfloat16
F32 = jnp.float32
Z, Y, C = 8, 2, 2
REPS = 8
BLK = 128
SLOTS = 16
F = 512
GROUPS = 8
DEG = 16
ROWS = 800
HALF = 144
PART = 8


def layer_perm(dz, dy, dc):
    pairs = []
    for z in range(Z):
        for y in range(Y):
            for c in range(C):
                to = (((z + dz) % Z) * Y + (y + dy) % Y) * C + (c + dc) % C
                pairs.append(((z * Y + y) * C + c, to))
    return pairs


def core_perm(hops):
    pairs = []
    for z in range(Z):
        for y in range(Y):
            for c in range(C):
                step = hops if c == 0 else -hops
                pairs.append(((z * Y + y) * C + c, (((z + step) % Z) * Y + y) * C + c))
    return pairs


OUT1, OUT2 = core_perm(1), core_perm(2)
BACK1, BACK2, BACK3, BACK4 = (core_perm(-hops) for hops in (1, 2, 3, 4))
SIDE = layer_perm(0, 1, 0)
CORE = layer_perm(0, 0, 1)

def send(value, perm):
    return lax.ppermute(value, "layer", perm)


def after(value, *earlier):
    return lax.optimization_barrier((value,) + earlier)[0]


def spread_kernel(first, place_ref, values_ref, *rest):
    dense_ref, degree_ref, tiles, sems = rest[-4:]
    step = pl.program_id(0)

    def fetch(p):
        return pltpu.make_async_copy(values_ref.at[first + p], tiles.at[p], sems.at[p])

    @pl.when(step == 0)
    def _():
        for p in range(PART):
            fetch(p).start()

    dense_ref[...] = jnp.zeros_like(dense_ref)
    fetch(step).wait()
    total = jnp.zeros((BLK, BLK), jnp.int32)
    for slot in reversed(range(SLOTS)):
        tile = tiles[step, slot]
        total = total + tile
        place = place_ref[(first + step) * SLOTS + slot]
        lane = pl.multiple_of((place % 4) * BLK, BLK)
        dense_ref[place // 4, :, pl.ds(lane, BLK)] = tile.astype(F32).astype(BF)

    row = lax.dot_general(
        jnp.ones((DEG, BLK), BF),
        total.astype(F32).astype(BF),
        (((1,), (1,)), ((), ())),
        preferred_element_type=F32,
    )
    high = jnp.floor(row * (1.0 / 128.0)) * 128.0
    degree_ref[...] = jnp.zeros_like(degree_ref)
    degree_ref[0, :, 0:BLK] = high.astype(BF)
    degree_ref[0, :, BLK : 2 * BLK] = (row - high).astype(BF)


def spread_part(place, values, first, dense=None):
    panels = values.shape[0]
    given = [] if dense is None else [dense]
    return pl.pallas_call(
        functools.partial(spread_kernel, first),
        grid_spec=pltpu.PrefetchScalarGridSpec(
            num_scalar_prefetch=1,
            grid=(PART,),
            in_specs=[pl.BlockSpec(memory_space=pltpu.HBM)]
            + [pl.BlockSpec(memory_space=pl.ANY)] * len(given),
            out_specs=[
                pl.BlockSpec((GROUPS, BLK, 4 * BLK), lambda p, place: (0, first + p, 0)),
                pl.BlockSpec((1, DEG, F), lambda p, place: (p, 0, 0)),
            ],
            scratch_shapes=[
                pltpu.VMEM((PART, SLOTS, BLK, BLK), jnp.int32),
                pltpu.SemaphoreType.DMA((PART,)),
            ],
        ),
        out_shape=[
            jax.ShapeDtypeStruct((GROUPS, panels * BLK, 4 * BLK), BF),
            jax.ShapeDtypeStruct((PART, DEG, F), BF),
        ],
        input_output_aliases={2: 0} if given else {},
        compiler_params=pltpu.CompilerParams(vmem_limit_bytes=16 << 20),
        cost_estimate=pl.CostEstimate(flops=1 << 21, bytes_accessed=8 << 20, transcendentals=0),
    )(place.reshape(-1), pltpu.with_memory_space_constraint(values, pltpu.HBM), *given)


def payload_kernel(total_ref, dense_ref, last_ref, degree_ref, out_ref):
    product = jnp.dot(dense_ref[0], last_ref[...], preferred_element_type=F32)
    whole = (total_ref[...] + product).astype(BF)
    for p in range(2):
        out_ref[p, 0:BLK, :] = whole[p * BLK : (p + 1) * BLK]
        out_ref[p, BLK : BLK + DEG, :] = degree_ref[p]


def payload_of(total, dense, group, last, degree_rows):
    return pl.pallas_call(
        payload_kernel,
        grid=(REPS // 2,),
        in_specs=[
            pl.BlockSpec((2 * BLK, F), lambda p: (p, 0)),
            pl.BlockSpec((1, 2 * BLK, 4 * BLK), lambda p: (group, p, 0)),
            pl.BlockSpec((4 * BLK, F), lambda p: (0, 0)),
            pl.BlockSpec((2, DEG, F), lambda p: (p, 0, 0)),
        ],
        out_specs=pl.BlockSpec((2, BLK + DEG, F), lambda p: (p, 0, 0)),
        out_shape=jax.ShapeDtypeStruct((REPS, BLK + DEG, F), BF),
        compiler_params=pltpu.CompilerParams(vmem_limit_bytes=8 << 20),
        cost_estimate=pl.CostEstimate(
            flops=2 * REPS * BLK * 4 * BLK * F, bytes_accessed=5 << 20, transcendentals=0
        ),
    )(total, dense, last, degree_rows)


def node_kernel(
    got_ref, features_ref, weight_ref, bias_ref, cotangent_ref, act_ref, out_ref, scaled_ref
):
    got = got_ref[...].astype(F32)
    summed = jnp.sum(got, axis=0)
    parts = summed[BLK : BLK + 1, :]
    degree_row = 1.0 + parts[:, 0:BLK] + parts[:, BLK : 2 * BLK]
    degree = jnp.transpose(jnp.broadcast_to(degree_row, (BLK, BLK)))
    degree = jnp.concatenate([degree] * 4, axis=1)
    aggregate = summed[0:BLK] + features_ref[...].astype(F32)
    hidden_wide = (aggregate / degree).astype(BF)
    weight = weight_ref[...]
    preact = jnp.dot(hidden_wide, weight, preferred_element_type=F32) + bias_ref[...]
    gate = jax.nn.sigmoid(preact)
    act_ref[...] = (preact * gate).astype(BF)
    slope = (cotangent_ref[...].astype(F32) * gate * (1.0 + preact * (1.0 - gate))).astype(BF)
    rows = lax.dot_general(slope, weight, (((1,), (1,)), ((), ())), preferred_element_type=F32)
    scaled = (rows / degree).astype(BF)
    scaled_t = jnp.transpose(scaled.astype(F32)).astype(BF)
    scaled_ref[...] = scaled_t
    hidden_t = jnp.transpose(hidden_wide.astype(F32)).astype(BF)
    grad = jnp.dot(hidden_t, slope, preferred_element_type=F32).astype(BF)
    bias = jnp.sum(slope.astype(F32), axis=0, keepdims=True).astype(BF)
    out_ref[:, 768:ROWS, :] = jnp.zeros((REPS, 32, BLK), BF)
    for peer in range(REPS):
        out_ref[peer, 0:512, :] = scaled_t
        for b in range(4):
            out_ref[peer, 512 + 64 * b : 576 + 64 * b, :] = grad[
                64 * peer : 64 * peer + 64, BLK * b : BLK * (b + 1)
            ]
            out_ref[peer, 768 + b : 769 + b, :] = bias[:, BLK * b : BLK * (b + 1)]


def node_step(got, features, weight, bias_row, cotangent):
    return pl.pallas_call(
        node_kernel,
        out_shape=[
            jax.ShapeDtypeStruct((BLK, F), BF),
            jax.ShapeDtypeStruct((REPS, ROWS, BLK), BF),
            jax.ShapeDtypeStruct((F, BLK), BF),
        ],
        compiler_params=pltpu.CompilerParams(vmem_limit_bytes=24 << 20),
        cost_estimate=pl.CostEstimate(
            flops=6 * BLK * F * F, bytes_accessed=4 << 20, transcendentals=BLK * F
        ),
    )(got, features, weight, bias_row.reshape(1, F), cotangent)


def product_kernel(groups, first, left_ref, dense_ref, *rest):
    step = pl.program_id(0)
    if first:
        wide_ref = rest[-1]

        @pl.when(step == 0)
        def _():
            for p in range(REPS):
                wide_ref[:, BLK * p : BLK * (p + 1)] = left_ref[p]
    else:
        wide_ref = left_ref
    whole = jnp.dot(wide_ref[...], dense_ref[0], preferred_element_type=F32)
    away_ref, mine_ref = rest[:2]
    for index, group in enumerate(groups):

        @pl.when(step == index)
        def _():
            if group == 7:
                away_ref[:, : 2 * BLK] = whole[:, 2 * BLK :].astype(BF)
                mine_ref[:, : 2 * BLK] = whole[:, : 2 * BLK]
            elif group == 0:
                for part in (0, 1):
                    own = 2 * part * BLK
                    here = slice(part * BLK, (part + 1) * BLK)
                    rest[2][:, here] = whole[:, own + BLK : own + 2 * BLK].astype(BF)
                    rest[3][:, here] = whole[:, own : own + BLK]
            elif group % 2:
                mine_ref[:, mine_ref.shape[1] - 4 * BLK :] = whole
            else:
                away_ref[:, away_ref.shape[1] - 4 * BLK :] = whole.astype(BF)


def products(left, dense, groups, first):
    columns = 6 * BLK if 7 in groups else 4 * BLK
    shapes = [((F, columns), BF), ((F, columns), F32)]
    if 0 in groups:
        shapes += [((F, 2 * BLK), BF), ((F, 2 * BLK), F32)]
    if first:
        shapes.append(((F, REPS * BLK), BF))
        left_spec = pl.BlockSpec((REPS, F, BLK), lambda i: (0, 0, 0))
    else:
        left_spec = pl.BlockSpec((F, REPS * BLK), lambda i: (0, 0))
    top = groups[0]
    return pl.pallas_call(
        functools.partial(product_kernel, groups, first),
        grid=(len(groups),),
        in_specs=[
            left_spec,
            pl.BlockSpec((1, REPS * BLK, 4 * BLK), lambda i: (top - i, 0, 0)),
        ],
        out_specs=[pl.BlockSpec(shape, lambda i: (0, 0)) for shape, _ in shapes],
        out_shape=[jax.ShapeDtypeStruct(shape, dtype) for shape, dtype in shapes],
        compiler_params=pltpu.CompilerParams(vmem_limit_bytes=20 << 20),
        cost_estimate=pl.CostEstimate(
            flops=len(groups) * 2 * F * REPS * BLK * 4 * BLK,
            bytes_accessed=len(groups) * (5 << 19),
            transcendentals=0,
        ),
    )(left, dense)


def forward(features, place_of, values):
    def dot(g, piece):
        return jnp.dot(dense[g], piece, preferred_element_type=F32)

    chain = jnp.concatenate([features, send(features, CORE)], axis=0)
    beside = send(features, SIDE)
    second = send(chain, OUT2)
    place = place_of(chain)
    early = place
    own = jnp.concatenate([chain, beside, send(beside, CORE)], axis=0)
    early = after(early, own)
    dense, degree_rows = spread_part(early, values, 0)
    first = send(own, OUT1)
    third = send(second, OUT1)
    total = dot(0, own)
    fourth = send(second[:BLK], OUT2)
    both2 = jnp.concatenate([second, send(second, SIDE)], axis=0)
    cross2 = send(both2, CORE)
    cross1 = send(first, CORE)
    both3 = jnp.concatenate([third, send(third, SIDE)], axis=0)
    both4 = jnp.concatenate([fourth, send(fourth, SIDE)], axis=0)
    total = total + dot(1, first) + dot(3, both2)
    total = total + dot(4, cross2) + dot(2, cross1)
    both4 = after(both4, total)
    last = jnp.concatenate([both4, send(both4, CORE)], axis=0)
    total = total + dot(7, last)
    both3 = after(both3, total)
    cross3 = send(both3, CORE)
    total = total + dot(5, both3)
    return payload_of(total, dense, 6, cross3, degree_rows), dense


def final_kernel(mine_ref, far_ref, near_ref, other_ref, scaled_ref, out_ref):
    total = (
        mine_ref[...]
        + far_ref[:, :BLK].astype(F32)
        + near_ref[:, :BLK].astype(F32)
        + other_ref[...].astype(F32)
        + scaled_ref[...].astype(F32)
    )
    out_ref[...] = jnp.transpose(total).astype(BF)


def final_step(*parts):
    return pl.pallas_call(
        final_kernel,
        out_shape=jax.ShapeDtypeStruct((BLK, F), BF),
        compiler_params=pltpu.CompilerParams(vmem_limit_bytes=8 << 20),
        cost_estimate=pl.CostEstimate(flops=1 << 19, bytes_accessed=1 << 20, transcendentals=0),
    )(*parts)


def gradient_kernel(pieces_ref, out_ref):
    for peer in range(REPS):
        for b in range(4):
            out_ref[64 * peer : 64 * peer + 64, BLK * b : BLK * (b + 1)] = pieces_ref[
                peer, 64 * b : 64 * b + 64
            ].astype(F32)


def gradient_of(pieces):
    return pl.pallas_call(
        gradient_kernel,
        out_shape=jax.ShapeDtypeStruct((F, F), F32),
        compiler_params=pltpu.CompilerParams(vmem_limit_bytes=8 << 20),
        cost_estimate=pl.CostEstimate(flops=1 << 18, bytes_accessed=3 << 19, transcendentals=0),
    )(pieces)


def folded(rows):
    half = rows.shape[0] // 2
    return jnp.concatenate([rows[:half], rows[half:]], axis=1)


def unfolded(rows):
    return jnp.concatenate([rows[:, :BLK], rows[:, BLK:]], axis=0)


def backward(everyone, dense, scaled_t):
    def wide_of(value):
        return value.astype(F32)

    def stacked(*parts):
        return jnp.concatenate([part.astype(BF) for part in parts], axis=0)

    grads = jnp.sum(wide_of(everyone[:, F:]), axis=0)
    grads = folded(grads + wide_of(send(grads.astype(BF), CORE)))
    away, mine, wide = products(everyone, dense, (7, 6, 5), True)
    line = mine + wide_of(send(away, CORE))
    side3 = stacked(line[:, 4 * BLK :], grads)
    got3 = wide_of(send(side3, SIDE))
    side4 = line[:, BLK : 2 * BLK].astype(BF)
    away, mine = products(wide, dense, (4, 3), False)
    line2 = mine + wide_of(after(send(away, CORE), side3))
    side2 = line2[:, 2 * BLK :].astype(BF)
    got4 = wide_of(send(side4, SIDE))
    got2 = wide_of(send(side2, SIDE))
    away1, mine1, away0, mine0 = products(after(wide, side3), dense, (2, 1, 0), False)
    line1 = mine1 + wide_of(send(away1, CORE))
    side1 = after(line1[:, 2 * BLK :].astype(BF), side2)
    got1 = wide_of(send(side1, SIDE))
    line0 = mine0 + wide_of(send(away0, CORE))
    side0 = after(line0[:, BLK:].astype(BF), side1)
    quad0 = line0[:, :BLK] + wide_of(send(side0, SIDE))

    grads = grads + got3[F:]
    quad3 = stacked(line[:, 2 * BLK : 4 * BLK] + got3[:F], grads)
    quad4 = stacked(line[:, :BLK] + got4, unfolded(grads))
    quad3 = after(quad3, side2)
    quad4 = after(quad4, side2)
    came3 = send(quad3, BACK1)
    came4 = send(quad4, BACK2)
    quad2 = line2[:, : 2 * BLK] + got2 + wide_of(came3[:F])
    quad2 = jnp.concatenate([quad2[:, :BLK] + wide_of(came4[:F]), quad2[:, BLK:]], axis=1)
    quad2 = quad2.astype(BF)
    far = send(quad2, BACK2)
    quad1 = (line1[:, : 2 * BLK] + got1).astype(BF)

    own = grads.astype(BF)
    own = after(own, quad3, quad4)
    third = send(own, BACK3)
    fourth = send(own, BACK4)
    around = wide_of(came3[F:]) + wide_of(folded(came4[F:]))
    around = around + wide_of(third) + 0.5 * wide_of(fourth)
    got = send(around, CORE)
    got = after(got, quad2)
    grads = grads + around + got

    quad1 = after(quad1, grads)
    near = send(quad1, BACK1)
    other = send((wide_of(far[:, BLK:]) + wide_of(near[:, BLK:])).astype(BF), CORE)
    return final_step(quad0, far, near, other, scaled_t), unfolded(grads)


def per_device(features, block_columns, block_values, weight, bias_row, cotangent):
    def place_of(chain):
        layer = lax.axis_index("layer")
        z, y, c = layer // 4, (layer // 2) % 2, layer % 2
        columns = after(block_columns, chain)
        owner = jnp.where(columns >= 0, columns, 0) // REPS
        dz = (owner // 4 - z + Z) % Z
        dy = ((owner // 2) % 2 - y) % 2
        dc = (owner % 2 - c) % 2
        near = jnp.where(dz <= 4, dz, Z - dz)
        other = ((dz > 4) != (c == 0)).astype(jnp.int32)
        ends = (near == 0) | (near == 4)
        group = jnp.where(near == 0, 0, jnp.where(near == 4, 7, 2 * near - 1 + other))
        column = jnp.where(near == 4, 2 * dc + dy, 2 * dy + jnp.where(ends, dc, dc ^ other))
        place = 4 * group + column
        return jnp.where(columns >= 0, place, place[:, 0:1]).astype(jnp.int32)

    payload, dense = forward(features, place_of, block_values)
    got = lax.all_to_all(payload, "rep", 0, 0, tiled=True)

    activations, outgoing, scaled_t = node_step(got, features, weight, bias_row, cotangent)
    everyone = lax.all_to_all(outgoing, "rep", 0, 0, tiled=True)
    feature_grad, grads = backward(everyone, dense, scaled_t)
    bias_grad = grads[256:260].reshape(F)
    mine = jnp.broadcast_to(grads[:256].astype(BF)[None], (REPS, 256, BLK))
    pieces = lax.all_to_all(mine, "rep", 0, 0, tiled=True)
    weight_grad = gradient_of(pieces)
    return (activations, weight_grad, bias_grad, feature_grad)


def solution(mesh):
    in_specs = (
        P(("layer", "rep"), None),
        P("layer", "rep"),
        P("layer", "rep", None, None),
        P(),
        P(),
        P(("layer", "rep"), None),
    )
    out_specs = (P(("layer", "rep"), None), P(), P(), P(("layer", "rep"), None))
    return jax.shard_map(
        per_device, mesh=mesh, in_specs=in_specs, out_specs=out_specs, check_vma=False
    )
```
